32 devices in a mesh: chan: 16 (over z, y, x), freq: 2 (over core).
Axes of the slice: x: 2, y: 2, z: 4, core: 2. Of those that a mesh axis runs over, the one named last changes fastest.
Arguments:
- spectra: bfloat16 [256, 2, 16, 2048], P('freq', None, None, 'chan'), may hold values from -20 to 20
- model: bfloat16 [256, 2, 8, 2048], P('freq', None, None, 'chan'), may hold values from -6 to 6
- channel_ok: int32 [2048], replicated, may hold values 0 or 1
- limits: int32 [16], replicated, may hold values from 128 to 1024, as said below
Outputs:
- adjoint: float32 [256, 2, 16, 2048], P('freq', None, None, 'chan')
- misfit: float32 [], replicated
The draws below stay inside these ranges and needn't reach their ends.
Inputs may be any that keep to these rules, and one draw needn't show every extreme that they name: `limits`: one block has the limit 128 and another the limit 1024.
All inputs are finite; a program needn't handle non-finite values.
Results may differ from the reference program's by a relative error of at most 0.00053.
Values may be sent and summed in bfloat16 or wider, within the bound.
No kernel may reach another device: no remote copies, remote signals or barrier semaphores. Data moves between devices by JAX's collectives and lax.ppermute only.
A program may use at most 192 MiB of HBM per device.

```python
import math
import jax
import jax.numpy as jnp
from jax import lax

F = 256
W = 16
K = 8
BAND = 1024
C_DEV = 128
CHANNELS = 2048


def channel_gain(key):
    position = jnp.arange(CHANNELS, dtype=jnp.float32) / CHANNELS
    reach = 0.4
    jitter = jax.random.uniform(jax.random.fold_in(key, 11), (CHANNELS,), jnp.float32, -reach, reach)
    return jnp.exp(jitter) * (1.0 + 0.6 * position)


def noise_field(key, salt, row_count, size):
    gain = channel_gain(key)
    noise_key = jax.random.fold_in(key, salt)
    values = jnp.clip(jax.random.normal(noise_key, (F, 2, row_count, CHANNELS), jnp.float32), -4.0, 4.0) * gain
    return values * size


def draw_spectra(key, part):
    return noise_field(key, 1, W, 1.0).astype(jnp.bfloat16)


def draw_model(key, part):
    return noise_field(key, 2, K, 0.3).astype(jnp.bfloat16)


def draw_limits(key, part):
    block_total = CHANNELS // C_DEV
    values = jax.random.randint(jax.random.fold_in(key, 21), (block_total,), C_DEV, BAND + 1, dtype=jnp.int32)
    chosen_order = jax.random.permutation(jax.random.fold_in(key, 22), block_total)
    values = values.at[chosen_order[0]].set(BAND)
    values = values.at[chosen_order[1]].set(C_DEV)
    return values


def place_ends(values, key, smallest, top_value):
    longest = values.shape.index(max(values.shape))
    spots = []
    for shift in (0, 1):
        where = [jax.random.randint(jax.random.fold_in(key, axis), (), 0, length) for axis, length in enumerate(values.shape)]
        where[longest] = (where[longest] + shift) % values.shape[longest]
        spots.append(tuple(where))
    return values.at[spots[0]].set(smallest).at[spots[1]].set(top_value)


def setup_inputs(seed: int = 0) -> dict:
    keys = jax.random.split(jax.random.key(seed), 5)
    return {
        "spectra": draw_spectra(jax.random.fold_in(keys[4], 71), 0),
        "model": draw_model(jax.random.fold_in(keys[4], 71), 0),
        "channel_ok": place_ends((jax.random.randint(keys[2], (CHANNELS,), 0, 16) < 15).astype(jnp.int32), jax.random.fold_in(keys[2], 1), 0, 1),
        "limits": draw_limits(jax.random.fold_in(keys[4], 71), 0),
    }


def complex_cross(left_rows, right_rows):
    real_part = jnp.einsum('grbc,grbd->gbcd', left_rows[:, 0], right_rows[:, 0]) + jnp.einsum('grbc,grbd->gbcd', left_rows[:, 1], right_rows[:, 1])
    imag_part = jnp.einsum('grbc,grbd->gbcd', left_rows[:, 1], right_rows[:, 0]) - jnp.einsum('grbc,grbd->gbcd', left_rows[:, 0], right_rows[:, 1])
    return real_part, imag_part


def reference(spectra, model, channel_ok, limits):
    band_blocks = BAND // C_DEV
    block_total = CHANNELS // C_DEV
    row_count = W + K
    group_size = math.gcd(F, 16)
    group_total = F // group_size
    row_scale = jnp.concatenate([jnp.full((W,), 1.0 / W, jnp.float32), jnp.full((K,), -1.0, jnp.float32)])
    payload = jnp.concatenate([spectra, model], axis=2).astype(jnp.float32)
    ok_all = channel_ok.astype(jnp.float32).reshape(block_total, C_DEV)
    row_index = jnp.arange(C_DEV, dtype=jnp.int32)[:, None]
    col_index = jnp.arange(C_DEV, dtype=jnp.int32)[None, :]

    def one_group(pay_rows):
        pay_blocks = pay_rows.reshape(group_size, 2, row_count, block_total, C_DEV)
        scaled = pay_blocks * row_scale[None, None, :, None, None]
        spec_blocks = pay_blocks[:, :, :W]
        adjoint_sum = jnp.zeros(spec_blocks.shape, jnp.float32)
        misfit_sum = jnp.zeros((), jnp.float32)
        for s in range(band_blocks + 1):
            partner = jnp.roll(pay_blocks, -s, axis=3)
            partner_spec = partner[:, :, :W]
            partner_ok = jnp.roll(ok_all, -s, axis=0)
            real_part, imag_part = complex_cross(scaled, partner)
            offset = s * C_DEV + col_index - row_index
            inside = ((offset >= 1) & (offset <= limits[:, None, None])).astype(jnp.float32)
            live_mask = ok_all[:, :, None] * partner_ok[:, None, :] * inside
            real_res = real_part * live_mask[None]
            imag_res = imag_part * live_mask[None]
            misfit_sum = misfit_sum + 0.5 * jnp.sum(real_res * real_res + imag_res * imag_res)
            real_round = lax.optimization_barrier(real_res.astype(jnp.bfloat16)).astype(jnp.float32)
            imag_round = lax.optimization_barrier(imag_res.astype(jnp.bfloat16)).astype(jnp.float32)
            own_real = jnp.einsum('gbcd,gwbd->gwbc', real_round, partner_spec[:, 0]) - jnp.einsum('gbcd,gwbd->gwbc', imag_round, partner_spec[:, 1])
            own_imag = jnp.einsum('gbcd,gwbd->gwbc', real_round, partner_spec[:, 1]) + jnp.einsum('gbcd,gwbd->gwbc', imag_round, partner_spec[:, 0])
            far_real = jnp.einsum('gbcd,gwbc->gwbd', real_round, spec_blocks[:, 0]) + jnp.einsum('gbcd,gwbc->gwbd', imag_round, spec_blocks[:, 1])
            far_imag = jnp.einsum('gbcd,gwbc->gwbd', real_round, spec_blocks[:, 1]) - jnp.einsum('gbcd,gwbc->gwbd', imag_round, spec_blocks[:, 0])
            far_part = jnp.roll(jnp.stack([far_real, far_imag], axis=1), s, axis=3)
            adjoint_sum = adjoint_sum + jnp.stack([own_real, own_imag], axis=1) + far_part
        return (adjoint_sum * (1.0 / W)).reshape(group_size, 2, W, CHANNELS), misfit_sum

    grouped = payload.reshape(group_total, group_size, 2, row_count, CHANNELS)
    adjoint_groups, misfit_groups = lax.map(one_group, grouped)
    adjoint = adjoint_groups.reshape(F, 2, W, CHANNELS)
    misfit = jnp.sum(misfit_groups) / float(F * CHANNELS * BAND)
    return adjoint, misfit
```

```python
import functools
import math

import jax
import jax.numpy as jnp
from jax import lax
from jax.experimental import pallas as pl
from jax.experimental.pallas import tpu as pltpu
from jax.sharding import PartitionSpec as P

W = 16
BAND = 1024
CHUNKS = 2


def band_kernel(limits_ref, x_ref, adj_ref, mis_ref, wt_ref, at_ref, acc_ref, *, firsts, wrap):
    blocks, bins, rows, width = x_ref.shape
    terms = (rows - 2 * W) // 2
    acc_ref[...] = jnp.zeros_like(acc_ref)
    adj_ref[...] = jnp.zeros_like(adj_ref)

    def prepare(b, carry):
        for f in range(bins):
            x = x_ref[b, f].astype(jnp.float32)
            sr, si, mr, mi = x[:W], x[W : 2 * W], x[2 * W : 2 * W + terms], x[2 * W + terms :]
            wt_ref[b, f, :, :width] = x.astype(jnp.bfloat16)
            wt_ref[b, f, :, width:] = jnp.concatenate([-si, sr, -mi, mr], axis=0).astype(jnp.bfloat16)
            scaled = jnp.concatenate([x[: 2 * W] * (1.0 / W), -x[2 * W :]], axis=0)
            at_ref[b, f] = scaled.T.astype(jnp.bfloat16)
        return carry

    lax.fori_loop(0, blocks, prepare, 0)

    row = lax.broadcasted_iota(jnp.int32, (width, 2 * width), 0)
    col = lax.broadcasted_iota(jnp.int32, (width, 2 * width), 1) % width
    diff = col - row

    def residual(b, j, f, mask, weight):
        w = wt_ref[j, f]
        r = jnp.dot(at_ref[b, f], w, preferred_element_type=jnp.float32)
        if mask is not None:
            r = jnp.where(mask, r, 0.0)
        squares = jnp.sum((r * r).reshape(width // 8, 8, 2 * width), axis=0)
        acc_ref[f] += squares * weight if weight != 1.0 else squares
        r = r.astype(jnp.bfloat16)
        own = lax.dot_general(w[: 2 * W], r, (((1,), (1,)), ((), ())), preferred_element_type=jnp.float32)
        adj_ref[b, f] += own
        return r

    def piece(b, s, mask):
        j = b + s
        if wrap:
            j = jnp.where(j >= blocks, j - blocks, j)
        for f in range(bins):
            r = residual(b, j, f, mask, 1.0)
            far = jnp.dot(wt_ref[b, f, : 2 * W, :width], r, preferred_element_type=jnp.float32)
            adj_ref[j, f, :W] += far[:W, :width] + far[W:, width:]
            adj_ref[j, f, W:] += far[W:, :width] - far[:W, width:]

    def block(b, carry):
        limit = limits_ref[b]
        for f in range(bins):
            residual(b, b, f, diff != 0, 0.5)

        def full(s, c):
            piece(b, s, None)
            return c

        def edge(s, c):
            piece(b, s, s * width + diff <= limit)
            return c

        first_edge = limit // width
        lax.fori_loop(1, first_edge, full, 0)
        lax.fori_loop(first_edge, (limit + width - 1) // width + 1, edge, 0)
        return carry

    lax.fori_loop(0, firsts, block, 0)
    adj_ref[...] = adj_ref[...] * (1.0 / W)
    mis_ref[0, 0] = jnp.sum(acc_ref[...])


def band_call(limits, x, firsts, wrap):
    blocks, bins, rows, width = x.shape
    return pl.pallas_call(
        functools.partial(band_kernel, firsts=firsts, wrap=wrap),
        out_shape=(
            jax.ShapeDtypeStruct((blocks, bins, 2 * W, width), jnp.float32),
            jax.ShapeDtypeStruct((1, 1), jnp.float32),
        ),
        in_specs=[pl.BlockSpec(memory_space=pltpu.SMEM), pl.BlockSpec(memory_space=pltpu.VMEM)],
        out_specs=(pl.BlockSpec(memory_space=pltpu.VMEM), pl.BlockSpec(memory_space=pltpu.SMEM)),
        scratch_shapes=[
            pltpu.VMEM((blocks, bins, rows, 2 * width), jnp.bfloat16),
            pltpu.VMEM((blocks, bins, width, rows), jnp.bfloat16),
            pltpu.VMEM((bins, 8, 2 * width), jnp.float32),
        ],
        compiler_params=pltpu.CompilerParams(vmem_limit_bytes=40 * 2**20),
        name="band",
    )(limits, x)


def shards(spectra, model, channel_ok, limits):
    bin_total, _, _, width = spectra.shape
    peers = lax.axis_size("chan")
    here = lax.axis_index("chan")
    band_blocks = BAND // width
    group = max(g for g in range(1, peers + 1) if peers % g == 0 and bin_total % g == 0)
    wrap = group == peers
    groups = [[start + i for i in range(group)] for start in range(0, peers, group)]
    per_device = bin_total // group
    chunks = math.gcd(CHUNKS, per_device)
    bins = per_device // chunks

    ok = lax.dynamic_slice_in_dim(channel_ok, here * width, width).astype(jnp.bfloat16)
    payload = (
        jnp.concatenate(
            [spectra.reshape(bin_total, -1, width), model.reshape(bin_total, -1, width)], axis=1
        )
        * ok
    )
    rows = payload.shape[1]
    chunk_bins = bin_total // chunks
    group_limits = lax.dynamic_slice_in_dim(limits, here // group * group, group)

    def swap(x):
        return lax.all_to_all(x, "chan", 0, 0, axis_index_groups=None if wrap else groups, tiled=True)

    def halo_move(x, by):
        return lax.ppermute(x, "chan", [(i, (i + by) % peers) for i in range(peers)])

    adjoint_parts = []
    misfit_sum = 0.0
    for c in range(chunks):
        part = swap(payload[c * chunk_bins : (c + 1) * chunk_bins]).reshape(group, bins, rows, width)
        if not wrap:
            part = jnp.concatenate([part, halo_move(part[:band_blocks], -group)], axis=0)
        adjoint, misfit = band_call(group_limits, part, group, wrap)
        if not wrap:
            back = halo_move(adjoint[group:], group)
            adjoint = jnp.concatenate([adjoint[:band_blocks] + back, adjoint[band_blocks:group]], axis=0)
        misfit_sum = misfit_sum + misfit[0, 0]
        adjoint_parts.append(swap(adjoint.reshape(chunk_bins, 2 * W, width)))
    adjoint = jnp.concatenate(adjoint_parts, axis=0).reshape(bin_total, 2, W, width)
    misfit = lax.psum(misfit_sum, ("chan", "freq"))
    return adjoint, misfit / float(2 * bin_total * lax.axis_size("freq") * peers * width * BAND)


def solution(mesh):
    return jax.shard_map(
        shards,
        mesh=mesh,
        in_specs=(P("freq", None, None, "chan"), P("freq", None, None, "chan"), P(), P()),
        out_specs=(P("freq", None, None, "chan"), P()),
        check_vma=False,
    )
```

```python
import functools
import math

import jax
import jax.numpy as jnp
from jax import lax
from jax.experimental import pallas as pl
from jax.experimental.pallas import tpu as pltpu
from jax.sharding import PartitionSpec as P

W = 16
BAND = 1024
CHUNKS = 2
UNROLL = 16
SCALE_ROWS = 16


def scaled_rows(adjoint):
    bins, rows, width = adjoint.shape
    top = jnp.maximum(jnp.max(jnp.abs(adjoint), axis=1, keepdims=True), 1e-30)
    exponent = jnp.ceil(jnp.log(top) * (1.0 / math.log(2.0)))
    scaled = adjoint * jnp.exp2(15.0 - exponent)
    exponents = jnp.zeros((SCALE_ROWS, width), jnp.float32)
    place = lax.broadcasted_iota(jnp.int32, (SCALE_ROWS, width), 0)
    for f in range(bins):
        exponents = jnp.where(place == f, exponent[f], exponents)
    return jnp.concatenate([scaled.reshape(bins * rows, width), exponents], axis=0)


def unscaled(packed, bins):
    blocks, _, width = packed.shape
    values = packed[:, : bins * 2 * W].astype(jnp.float32).reshape(blocks, bins, 2 * W, width)
    exponents = packed[:, bins * 2 * W : bins * 2 * W + bins].astype(jnp.float32)
    return values * jnp.exp2(exponents - 15.0)[:, :, None]


def band_kernel(limits_ref, ok_ref, x_ref, out_ref, mis_ref, wt_ref, at_ref, acc_ref, own_ref, far_ref, r0_ref, r1_ref, *, firsts, wrap, pack):
    blocks, bins, rows, width = x_ref.shape
    terms = (rows - 2 * W) // 2
    unroll = max(2, UNROLL // bins // 2 * 2)
    slots = (r0_ref, r1_ref)
    acc_ref[...] = jnp.zeros_like(acc_ref)

    def prepare(b, carry):
        ok = ok_ref[b].astype(jnp.float32)
        for f in range(bins):
            x = x_ref[b, f].astype(jnp.float32) * ok
            sr, si, mr, mi = x[:W], x[W : 2 * W], x[2 * W : 2 * W + terms], x[2 * W + terms :]
            wt_ref[b, f, :, :width] = x.astype(jnp.bfloat16)
            wt_ref[b, f, :, width:] = jnp.concatenate([-si, sr, -mi, mr], axis=0).astype(jnp.bfloat16)
            scaled = jnp.concatenate([x[: 2 * W] * (1.0 / W), -x[2 * W :]], axis=0)
            at_ref[b, f] = scaled.T.astype(jnp.bfloat16)
        own_ref[b] = jnp.zeros_like(own_ref[b])
        far_ref[b] = jnp.zeros_like(far_ref[b])
        return carry

    lax.fori_loop(0, blocks, prepare, 0)

    row = lax.broadcasted_iota(jnp.int32, (width, 2 * width), 0)
    col = lax.broadcasted_iota(jnp.int32, (width, 2 * width), 1) % width
    diff = col - row

    def last_piece(b):
        return (limits_ref[b] + width - 1) // width

    def next_item(b, s):
        done = (b >= firsts) | (s >= last_piece(jnp.minimum(b, firsts - 1)))
        return jnp.where(done, b + 1, b), jnp.where(done, 0, s + 1)

    def blocks_of(b, s):
        b = jnp.minimum(b, firsts - 1)
        j = b + s
        if wrap:
            j = jnp.where(j >= blocks, j - blocks, j)
        return b, j

    def cross(slot, item):
        b, s = item
        low = jnp.where(b < firsts, jnp.where(s == 0, 1, -width), width)
        b, j = blocks_of(b, s)
        mask = (diff >= low) & (diff <= limits_ref[b] - s * width)
        for f in range(bins):
            r = jnp.dot(at_ref[b, f], wt_ref[j, f], preferred_element_type=jnp.float32)
            r = jnp.where(mask, r, 0.0)
            acc_ref[f] += jnp.sum((r * r).reshape(width // 8, 8, 2 * width), axis=0)
            slots[slot][f] = r.astype(jnp.bfloat16)

    def adjoint(slot, item):
        b, j = blocks_of(*item)
        for f in range(bins):
            r = slots[slot][f]
            own_ref[b, f] += lax.dot_general(
                wt_ref[j, f, : 2 * W], r, (((1,), (1,)), ((), ())), preferred_element_type=jnp.float32
            )
            far = jnp.dot(wt_ref[b, f, : 2 * W, :width], r, preferred_element_type=jnp.float32)
            far_ref[j, f, :W] += far[:W, :width] + far[W:, width:]
            far_ref[j, f, W:] += far[W:, :width] - far[:W, width:]

    def step(_, item):
        for i in range(unroll):
            later = next_item(*item)
            cross((i + 1) % 2, later)
            adjoint(i % 2, item)
            item = later
        return item

    total = lax.fori_loop(0, firsts, lambda b, n: n + last_piece(b) + 1, jnp.int32(0))
    first = (jnp.int32(0), jnp.int32(0))
    cross(0, first)
    lax.fori_loop(0, (total + unroll - 1) // unroll, step, first)

    def finish(b, carry):
        result = (own_ref[b] + far_ref[b]) * (1.0 / W)
        out_ref[b] = scaled_rows(result) if pack else result
        return carry

    lax.fori_loop(0, blocks, finish, 0)
    mis_ref[0, 0] = jnp.sum(acc_ref[...])


def band_call(limits, ok, x, firsts, wrap, pack):
    blocks, bins, rows, width = x.shape
    out_shape = (blocks, bins * 2 * W + SCALE_ROWS, width) if pack else (blocks, bins, 2 * W, width)
    vmem = pl.BlockSpec(memory_space=pltpu.VMEM)
    smem = pl.BlockSpec(memory_space=pltpu.SMEM)
    return pl.pallas_call(
        functools.partial(band_kernel, firsts=firsts, wrap=wrap, pack=pack),
        out_shape=(
            jax.ShapeDtypeStruct(out_shape, jnp.float32),
            jax.ShapeDtypeStruct((1, 1), jnp.float32),
        ),
        in_specs=[smem, vmem, vmem],
        out_specs=(vmem, smem),
        scratch_shapes=[
            pltpu.VMEM((blocks, bins, rows, 2 * width), jnp.bfloat16),
            pltpu.VMEM((blocks, bins, width, rows), jnp.bfloat16),
            pltpu.VMEM((bins, 8, 2 * width), jnp.float32),
            pltpu.VMEM((blocks, bins, 2 * W, width), jnp.float32),
            pltpu.VMEM((blocks, bins, 2 * W, width), jnp.float32),
            pltpu.VMEM((bins, width, 2 * width), jnp.bfloat16),
            pltpu.VMEM((bins, width, 2 * width), jnp.bfloat16),
        ],
        compiler_params=pltpu.CompilerParams(vmem_limit_bytes=40 * 2**20),
        name="band",
    )(limits, ok, x)


def sum_over(x, axes):
    for axis in axes:
        peers = lax.axis_size(axis)
        if peers & (peers - 1):
            x = lax.psum(x, axis)
            continue
        reach = 1
        while reach < peers:
            x = x + lax.ppermute(x, axis, [(i, i ^ reach) for i in range(peers)])
            reach *= 2
    return x


def shards(spectra, model, channel_ok, limits):
    bin_total, _, _, width = spectra.shape
    peers = lax.axis_size("chan")
    here = lax.axis_index("chan")
    band_blocks = BAND // width
    group = max(g for g in range(1, peers + 1) if peers % g == 0 and bin_total % g == 0)
    wrap = group == peers
    groups = None if wrap else [[start + i for i in range(group)] for start in range(0, peers, group)]
    per_device = bin_total // group
    chunks = math.gcd(CHUNKS, per_device)
    bins = per_device // chunks
    chunk_bins = bin_total // chunks

    ok = channel_ok.reshape(peers, 1, width)
    if not wrap:
        start = here // group * group
        limits = lax.dynamic_slice_in_dim(limits, start, group)
        ok = lax.dynamic_slice_in_dim(jnp.concatenate([ok, ok]), start, group + band_blocks)
    payload = jnp.concatenate(
        [spectra.reshape(bin_total, -1, width), model.reshape(bin_total, -1, width)], axis=1
    )
    rows = payload.shape[1]

    def swap(x):
        return lax.all_to_all(x, "chan", 0, 0, axis_index_groups=groups, tiled=True)

    def halo_move(x, by):
        return lax.ppermute(x, "chan", [(i, (i + by) % peers) for i in range(peers)])

    adjoint_parts = []
    misfit_sum = 0.0
    for c in range(chunks):
        part = swap(payload[c * chunk_bins : (c + 1) * chunk_bins]).reshape(group, bins, rows, width)
        if not wrap:
            part = jnp.concatenate([part, halo_move(part[:band_blocks], -group)], axis=0)
        packed, misfit = band_call(limits, ok, part, group, wrap, wrap)
        if not wrap:
            back = halo_move(packed[group:], group)
            packed = jnp.concatenate([packed[:band_blocks] + back, packed[band_blocks:group]], axis=0)
            packed = jax.vmap(scaled_rows)(packed)
        misfit_sum = misfit_sum + misfit
        packed = swap(packed.astype(jnp.float16))
        adjoint_parts.append(unscaled(packed, bins).reshape(chunk_bins, 2, W, width))
    adjoint = jnp.concatenate(adjoint_parts, axis=0)
    misfit = sum_over(misfit_sum, ("freq", "chan"))[0, 0]
    return adjoint, misfit / float(2 * bin_total * lax.axis_size("freq") * peers * width * BAND)


def solution(mesh):
    return jax.shard_map(
        shards,
        mesh=mesh,
        in_specs=(P("freq", None, None, "chan"), P("freq", None, None, "chan"), P(), P()),
        out_specs=(P("freq", None, None, "chan"), P()),
        check_vma=False,
    )
```

```python
import functools
import math

import jax
import jax.numpy as jnp
from jax import lax
from jax.experimental import pallas as pl
from jax.experimental.pallas import tpu as pltpu
from jax.sharding import PartitionSpec as P

W = 16
BAND = 1024
CHUNKS = 2
UNROLL = 16
SELF_UNROLL = 16
EXTRA_ROWS = 16
MISFIT_ROWS = 4


def power_below(top):
    return jnp.ceil(jnp.log(jnp.maximum(top, 1e-30)) * (1.0 / math.log(2.0)))


def scaled_rows(adjoint, misfit):
    bins, rows, width = adjoint.shape
    exponent = power_below(jnp.max(jnp.abs(adjoint), axis=1, keepdims=True))
    scaled = adjoint * jnp.exp2(15.0 - exponent)
    misfit = jnp.sum(misfit, axis=0, keepdims=True)
    misfit = misfit[:, :width] + misfit[:, width:]
    power = power_below(misfit)
    rest = misfit * jnp.exp2(10.0 - power)
    lines = [exponent[f] for f in range(bins)]
    lines += [jnp.zeros_like(misfit)] * (EXTRA_ROWS - MISFIT_ROWS - bins) + [power]
    for _ in range(2):
        lines.append(jnp.floor(rest))
        rest = (rest - jnp.floor(rest)) * 1024.0
    lines.append(rest)
    place = lax.broadcasted_iota(jnp.int32, (EXTRA_ROWS, width), 0)
    extra = jnp.zeros((EXTRA_ROWS, width), jnp.float32)
    for n, line in enumerate(lines):
        extra = jnp.where(place == n, line, extra)
    return jnp.concatenate([scaled.reshape(bins * rows, width), extra], axis=0)


def unscaled(packed, bins):
    blocks, _, width = packed.shape
    values = packed[:, : bins * 2 * W].astype(jnp.float32).reshape(blocks, bins, 2 * W, width)
    exponents = packed[:, bins * 2 * W : bins * 2 * W + bins].astype(jnp.float32)
    return values * jnp.exp2(exponents - 15.0)[:, :, None]


def unscaled_misfit(packed):
    power, high, middle, low = [packed[:, n - MISFIT_ROWS].astype(jnp.float32) for n in range(MISFIT_ROWS)]
    return jnp.sum((high + middle * 2.0**-10 + low * 2.0**-20) * jnp.exp2(power - 10.0))


def expanded(x):
    terms = (x.shape[0] - 2 * W) // 2
    sr, si, mr, mi = x[:W], x[W : 2 * W], x[2 * W : 2 * W + terms], x[2 * W + terms :]
    turned = jnp.concatenate([-si, sr, -mi, mr], axis=0)
    scaled = jnp.concatenate([x[: 2 * W] * (1.0 / W), -x[2 * W :]], axis=0)
    return x.astype(jnp.bfloat16), turned.astype(jnp.bfloat16), scaled.T.astype(jnp.bfloat16)


def squares(r):
    return jnp.sum((r * r).reshape(r.shape[0] // 8, 8, r.shape[1]), axis=0)


def apply_rows(w, r):
    return lax.dot_general(w[: 2 * W], r, (((1,), (1,)), ((), ())), preferred_element_type=jnp.float32)


def self_kernel(ok_ref, x_ref, out_ref, mis_ref, *, unroll):
    bin_total, rows, width = x_ref.shape
    row = lax.broadcasted_iota(jnp.int32, (width, 2 * width), 0)
    col = lax.broadcasted_iota(jnp.int32, (width, 2 * width), 1) % width
    ok = ok_ref[...].astype(jnp.float32)
    mis_ref[...] = jnp.zeros_like(mis_ref)

    def step(t, carry):
        total = jnp.zeros(mis_ref.shape, jnp.float32)
        for i in range(unroll):
            f = t * unroll + i
            x, turned, left = expanded(x_ref[f].astype(jnp.float32) * ok)
            w = jnp.concatenate([x, turned], axis=1)
            r = jnp.dot(left, w, preferred_element_type=jnp.float32)
            r = jnp.where(row != col, r, 0.0)
            total += squares(r)
            out_ref[f] = apply_rows(w, r.astype(jnp.bfloat16)) * (1.0 / W)
        mis_ref[...] += total * 0.5
        return carry

    lax.fori_loop(0, bin_total // unroll, step, 0)


def self_call(ok, x):
    bin_total, rows, width = x.shape
    vmem = pl.BlockSpec(memory_space=pltpu.VMEM)
    return pl.pallas_call(
        functools.partial(self_kernel, unroll=math.gcd(bin_total, SELF_UNROLL)),
        out_shape=(
            jax.ShapeDtypeStruct((bin_total, 2 * W, width), jnp.float32),
            jax.ShapeDtypeStruct((8, 2 * width), jnp.float32),
        ),
        in_specs=[vmem, vmem],
        out_specs=(vmem, vmem),
        compiler_params=pltpu.CompilerParams(vmem_limit_bytes=40 * 2**20),
        name="own_block",
    )(ok, x)


def band_kernel(limits_ref, ok_ref, before_ref, x_ref, out_ref, mis_ref, wt_ref, at_ref, acc_ref, own_ref, far_ref, r0_ref, r1_ref, *, firsts, wrap, pack):
    blocks, bins, rows, width = x_ref.shape
    unroll = max(2, UNROLL // bins // 2 * 2)
    slots = (r0_ref, r1_ref)
    acc_ref[...] = jnp.zeros_like(acc_ref)

    def prepare(b, carry):
        ok = ok_ref[b].astype(jnp.float32)
        for f in range(bins):
            x, turned, left = expanded(x_ref[b, f].astype(jnp.float32) * ok)
            wt_ref[b, f, :, :width] = x
            wt_ref[b, f, :, width:] = turned
            at_ref[b, f] = left
        own_ref[b] = jnp.zeros_like(own_ref[b])
        far_ref[b] = jnp.zeros_like(far_ref[b])
        return carry

    lax.fori_loop(0, blocks, prepare, 0)

    row = lax.broadcasted_iota(jnp.int32, (width, 2 * width), 0)
    col = lax.broadcasted_iota(jnp.int32, (width, 2 * width), 1) % width
    diff = col - row

    def last_piece(b):
        return (limits_ref[b] + width - 1) // width

    def next_item(b, s):
        done = (b >= firsts) | (s >= last_piece(jnp.minimum(b, firsts - 1)))
        return jnp.where(done, b + 1, b), jnp.where(done, 1, s + 1)

    def blocks_of(b, s):
        b = jnp.minimum(b, firsts - 1)
        j = b + s
        if wrap:
            j = jnp.where(j >= blocks, j - blocks, j)
        return b, j

    def cross(slot, item):
        b, s = item
        live = b < firsts
        b, j = blocks_of(b, s)
        mask = diff <= jnp.where(live, limits_ref[b] - s * width, -width)
        for f in range(bins):
            r = jnp.dot(at_ref[b, f], wt_ref[j, f], preferred_element_type=jnp.float32)
            r = jnp.where(mask, r, 0.0)
            acc_ref[f] += squares(r)
            slots[slot][f] = r.astype(jnp.bfloat16)

    def adjoint(slot, item):
        b, j = blocks_of(*item)
        for f in range(bins):
            r = slots[slot][f]
            own_ref[b, f] += apply_rows(wt_ref[j, f], r)
            far = jnp.dot(wt_ref[b, f, : 2 * W, :width], r, preferred_element_type=jnp.float32)
            far_ref[j, f, :W] += far[:W, :width] + far[W:, width:]
            far_ref[j, f, W:] += far[W:, :width] - far[:W, width:]

    def step(_, item):
        for i in range(unroll):
            later = next_item(*item)
            cross((i + 1) % 2, later)
            adjoint(i % 2, item)
            item = later
        return item

    total = lax.fori_loop(0, firsts, lambda b, n: n + last_piece(b), jnp.int32(0))
    first = (jnp.int32(0), jnp.int32(1))
    cross(0, first)
    lax.fori_loop(0, (total + unroll - 1) // unroll, step, first)

    mis_ref[...] = before_ref[...] + jnp.sum(acc_ref[...], axis=0)

    def finish(b, carry):
        result = (own_ref[b] + far_ref[b]) * (1.0 / W)
        out_ref[b] = scaled_rows(result, mis_ref[...]) if pack else result
        return carry

    lax.fori_loop(0, blocks, finish, 0)


def band_call(limits, ok, before, x, firsts, wrap, pack):
    blocks, bins, rows, width = x.shape
    out_shape = (blocks, bins * 2 * W + EXTRA_ROWS, width) if pack else (blocks, bins, 2 * W, width)
    vmem = pl.BlockSpec(memory_space=pltpu.VMEM)
    smem = pl.BlockSpec(memory_space=pltpu.SMEM)
    return pl.pallas_call(
        functools.partial(band_kernel, firsts=firsts, wrap=wrap, pack=pack),
        out_shape=(
            jax.ShapeDtypeStruct(out_shape, jnp.float32),
            jax.ShapeDtypeStruct(before.shape, jnp.float32),
        ),
        in_specs=[smem, vmem, vmem, vmem],
        out_specs=(vmem, vmem),
        scratch_shapes=[
            pltpu.VMEM((blocks, bins, rows, 2 * width), jnp.bfloat16),
            pltpu.VMEM((blocks, bins, width, rows), jnp.bfloat16),
            pltpu.VMEM((bins, 8, 2 * width), jnp.float32),
            pltpu.VMEM((blocks, bins, 2 * W, width), jnp.float32),
            pltpu.VMEM((blocks, bins, 2 * W, width), jnp.float32),
            pltpu.VMEM((bins, width, 2 * width), jnp.bfloat16),
            pltpu.VMEM((bins, width, 2 * width), jnp.bfloat16),
        ],
        compiler_params=pltpu.CompilerParams(vmem_limit_bytes=40 * 2**20),
        name="band",
    )(limits, ok, before, x)


def sum_over(x, axis, reach=1):
    peers = lax.axis_size(axis)
    if reach == peers:
        return x
    if (peers // reach) & (peers // reach - 1):
        return lax.psum(x, axis) / reach
    while reach < peers:
        x = x + lax.ppermute(x, axis, [(i, i // (2 * reach) * 2 * reach + (i + reach) % (2 * reach)) for i in range(peers)])
        reach *= 2
    return x


def shards(spectra, model, channel_ok, limits):
    bin_total, _, _, width = spectra.shape
    peers = lax.axis_size("chan")
    here = lax.axis_index("chan")
    band_blocks = BAND // width
    group = max(g for g in range(1, peers + 1) if peers % g == 0 and bin_total % g == 0)
    wrap = group == peers
    groups = None if wrap else [[start + i for i in range(group)] for start in range(0, peers, group)]
    per_device = bin_total // group
    chunks = math.gcd(CHUNKS, per_device)
    bins = per_device // chunks
    chunk_bins = bin_total // chunks

    ok = channel_ok.reshape(peers, 1, width)
    ok_here = lax.dynamic_index_in_dim(ok, here, keepdims=False)
    if not wrap:
        start = here // group * group
        limits = lax.dynamic_slice_in_dim(limits, start, group)
        ok = lax.dynamic_slice_in_dim(jnp.concatenate([ok, ok]), start, group + band_blocks)
    payload = jnp.concatenate(
        [spectra.reshape(bin_total, -1, width), model.reshape(bin_total, -1, width)], axis=1
    )
    rows = payload.shape[1]

    def swap(x):
        return lax.all_to_all(x, "chan", 0, 0, axis_index_groups=groups, tiled=True)

    def halo_move(x, by):
        return lax.ppermute(x, "chan", [(i, (i + by) % peers) for i in range(peers)])

    adjoint, misfit = self_call(ok_here, payload)
    inbound = [payload[c * chunk_bins : (c + 1) * chunk_bins] for c in range(chunks)]
    after = misfit
    for c in range(chunks):
        if c:
            inbound[c], after = lax.optimization_barrier((inbound[c], after))
        inbound[c] = swap(inbound[c])
    outbound = []
    for c in range(chunks):
        part = inbound[c]
        if c:
            part, outbound[-1] = lax.optimization_barrier((part, outbound[-1]))
        part = part.reshape(group, bins, rows, width)
        if not wrap:
            part = jnp.concatenate([part, halo_move(part[:band_blocks], -group)], axis=0)
        packed, misfit = band_call(limits, ok, misfit, part, group, wrap, wrap)
        if not wrap:
            back = halo_move(packed[group:], group)
            packed = jnp.concatenate([packed[:band_blocks] + back, packed[band_blocks:group]], axis=0)
            packed = jax.vmap(scaled_rows, (0, None))(packed, misfit)
        outbound.append(packed.astype(jnp.float16))
    for c in range(chunks):
        packed = outbound[c]
        if c:
            packed, arrived = lax.optimization_barrier((packed, arrived))
        packed = swap(packed)
        arrived = packed
        part = unscaled(packed, bins).reshape(chunk_bins, 2 * W, width)
        part = part + lax.slice_in_dim(adjoint, c * chunk_bins, (c + 1) * chunk_bins)
        adjoint = lax.dynamic_update_slice_in_dim(adjoint, part, c * chunk_bins, 0)
    misfit = sum_over(sum_over(unscaled_misfit(packed), "freq"), "chan", group)
    misfit = misfit / float(2 * bin_total * lax.axis_size("freq") * peers * width * BAND)
    return adjoint.reshape(spectra.shape), misfit


def solution(mesh):
    return jax.shard_map(
        shards,
        mesh=mesh,
        in_specs=(P("freq", None, None, "chan"), P("freq", None, None, "chan"), P(), P()),
        out_specs=(P("freq", None, None, "chan"), P()),
        check_vma=False,
    )
```

```python
import functools
import math

import jax
import jax.numpy as jnp
from jax import lax
from jax.experimental import pallas as pl
from jax.experimental.pallas import tpu as pltpu
from jax.sharding import PartitionSpec as P

W = 16
BAND = 1024
CHUNKS = 2
UNROLL = 32
REST = 16
SELF_UNROLL = 16
EXTRA_ROWS = 8
MISFIT_ROWS = 4


def power_below(top):
    return jnp.ceil(jnp.log(jnp.maximum(top, 1e-30)) * (1.0 / math.log(2.0)))


def scaled_rows(adjoint, misfit):
    bins, rows, width = adjoint.shape
    exponent = power_below(jnp.max(jnp.abs(adjoint), axis=1, keepdims=True))
    scaled = adjoint * jnp.exp2(15.0 - exponent)
    misfit = jnp.sum(misfit, axis=0, keepdims=True)
    misfit = misfit[:, :width] + misfit[:, width:]
    power = power_below(misfit)
    rest = misfit * jnp.exp2(10.0 - power)
    lines = [exponent[f] for f in range(bins)]
    lines += [jnp.zeros_like(misfit)] * (EXTRA_ROWS - MISFIT_ROWS - bins) + [power]
    for _ in range(2):
        lines.append(jnp.floor(rest))
        rest = (rest - jnp.floor(rest)) * 1024.0
    lines.append(rest)
    place = lax.broadcasted_iota(jnp.int32, (EXTRA_ROWS, width), 0)
    extra = jnp.zeros((EXTRA_ROWS, width), jnp.float32)
    for n, line in enumerate(lines):
        extra = jnp.where(place == n, line, extra)
    return jnp.concatenate([scaled.reshape(bins * rows, width), extra], axis=0)


def unscaled(packed, bins):
    blocks, _, width = packed.shape
    values = packed[:, : bins * 2 * W].astype(jnp.float32).reshape(blocks, bins, 2 * W, width)
    exponents = packed[:, bins * 2 * W : bins * 2 * W + bins].astype(jnp.float32)
    return values * jnp.exp2(exponents - 15.0)[:, :, None]


def unscaled_misfit(packed):
    power, high, middle, low = [packed[:, n - MISFIT_ROWS].astype(jnp.float32) for n in range(MISFIT_ROWS)]
    return jnp.sum((high + middle * 2.0**-10 + low * 2.0**-20) * jnp.exp2(power - 10.0))


def expanded(x):
    terms = (x.shape[0] - 2 * W) // 2
    sr, si, mr, mi = x[:W], x[W : 2 * W], x[2 * W : 2 * W + terms], x[2 * W + terms :]
    turned = jnp.concatenate([-si, sr, -mi, mr], axis=0)
    scaled = jnp.concatenate([x[: 2 * W] * (1.0 / W), -x[2 * W :]], axis=0)
    return x.astype(jnp.bfloat16), turned.astype(jnp.bfloat16), scaled.T.astype(jnp.bfloat16)


def squares(r):
    return jnp.sum((r * r).reshape(r.shape[0] // 8, 8, r.shape[1]), axis=0)


def apply_rows(w, r):
    return lax.dot_general(w[: 2 * W], r, (((1,), (1,)), ((), ())), preferred_element_type=jnp.float32)


def self_kernel(ok_ref, spectra_ref, model_ref, out_ref, mis_ref, *, unroll):
    bin_total, _, width = spectra_ref.shape
    row = lax.broadcasted_iota(jnp.int32, (width, 2 * width), 0)
    col = lax.broadcasted_iota(jnp.int32, (width, 2 * width), 1) % width
    ok = ok_ref[...].astype(jnp.float32)
    mis_ref[...] = jnp.zeros_like(mis_ref)

    def step(t, carry):
        total = jnp.zeros(mis_ref.shape, jnp.float32)
        for i in range(unroll):
            f = t * unroll + i
            x = jnp.concatenate([spectra_ref[f].astype(jnp.float32), model_ref[f].astype(jnp.float32)], axis=0) * ok
            x, turned, left = expanded(x)
            w = jnp.concatenate([x, turned], axis=1)
            r = jnp.dot(left, w, preferred_element_type=jnp.float32)
            r = jnp.where(row != col, r, 0.0)
            total += squares(r)
            out_ref[f] = apply_rows(w, r.astype(jnp.bfloat16)) * (1.0 / W)
        mis_ref[...] += total * 0.5
        return carry

    lax.fori_loop(0, bin_total // unroll, step, 0)


def self_call(ok, spectra, model):
    bin_total, _, width = spectra.shape
    vmem = pl.BlockSpec(memory_space=pltpu.VMEM)
    return pl.pallas_call(
        functools.partial(self_kernel, unroll=math.gcd(bin_total, SELF_UNROLL)),
        out_shape=(
            jax.ShapeDtypeStruct((bin_total, 2 * W, width), jnp.float32),
            jax.ShapeDtypeStruct((8, 2 * width), jnp.float32),
        ),
        in_specs=[vmem, vmem, vmem],
        out_specs=(vmem, vmem),
        compiler_params=pltpu.CompilerParams(vmem_limit_bytes=40 * 2**20),
        name="own_block",
    )(ok, spectra, model)


def band_kernel(limits_ref, ok_ref, before_ref, x_ref, out_ref, mis_ref, wt_ref, at_ref, acc_ref, own_ref, far_ref, r0_ref, r1_ref, t0_ref, t1_ref, *, firsts, wrap, pack):
    blocks, bins, rows, width = x_ref.shape
    unroll = max(2, UNROLL // bins // 2 * 2)
    rest = max(2, REST // bins // 2 * 2)
    slots = (r0_ref, r1_ref)
    turned_slots = (t0_ref, t1_ref)
    acc_ref[...] = jnp.zeros_like(acc_ref)

    def prepare(b, carry):
        ok = ok_ref[b].astype(jnp.float32)
        for f in range(bins):
            x, turned, left = expanded(x_ref[b, f].astype(jnp.float32) * ok)
            wt_ref[b, f, :, :width] = x
            wt_ref[b, f, :, width:] = turned
            at_ref[b, f] = left
        own_ref[b] = jnp.zeros_like(own_ref[b])
        far_ref[b] = jnp.zeros_like(far_ref[b])
        return carry

    lax.fori_loop(0, blocks, prepare, 0, unroll=math.gcd(blocks, 4))

    row = lax.broadcasted_iota(jnp.int32, (width, 2 * width), 0)
    col = lax.broadcasted_iota(jnp.int32, (width, 2 * width), 1) % width
    diff = col - row

    def last_piece(b):
        return (limits_ref[b] + width - 1) // width

    def next_item(b, s):
        done = (b >= firsts) | (s >= last_piece(jnp.minimum(b, firsts - 1)))
        return jnp.where(done, b + 1, b), jnp.where(done, 1, s + 1)

    def blocks_of(b, s):
        b = jnp.minimum(b, firsts - 1)
        j = b + s
        if wrap:
            j = jnp.where(j >= blocks, j - blocks, j)
        return b, j

    def cross(slot, item):
        b, s = item
        live = b < firsts
        b, j = blocks_of(b, s)
        mask = diff <= jnp.where(live, limits_ref[b] - s * width, -width)
        for f in range(bins):
            r = jnp.dot(at_ref[b, f], wt_ref[j, f], preferred_element_type=jnp.float32)
            r = jnp.where(mask, r, 0.0)
            acc_ref[f] += squares(r)
            r = r.astype(jnp.bfloat16)
            slots[slot][f] = r
            if f % 2:
                turned_slots[slot][f, :, :width] = r[:, :width].T
                turned_slots[slot][f, :, width:] = r[:, width:].T

    def adjoint(slot, item):
        b, j = blocks_of(*item)
        for f in range(bins):
            r = slots[slot][f]
            if f % 2:
                own = jnp.dot(wt_ref[j, f, : 2 * W, :width], turned_slots[slot][f], preferred_element_type=jnp.float32)
                own_ref[b, f, :W] += own[:W, :width] - own[W:, width:]
                own_ref[b, f, W:] += own[W:, :width] + own[:W, width:]
            else:
                own_ref[b, f] += apply_rows(wt_ref[j, f], r)
            far = jnp.dot(wt_ref[b, f, : 2 * W, :width], r, preferred_element_type=jnp.float32)
            far_ref[j, f, :W] += far[:W, :width] + far[W:, width:]
            far_ref[j, f, W:] += far[W:, :width] - far[:W, width:]

    def step(count, _, item):
        for i in range(count):
            later = next_item(*item)
            cross((i + 1) % 2, later)
            adjoint(i % 2, item)
            item = later
        return item

    total = lax.fori_loop(0, firsts, lambda b, n: n + last_piece(b), jnp.int32(0))
    first = (jnp.int32(0), jnp.int32(1))
    cross(0, first)
    if rest == unroll:
        lax.fori_loop(0, (total + unroll - 1) // unroll, functools.partial(step, unroll), first)
    else:
        item = lax.fori_loop(0, total // unroll, functools.partial(step, unroll), first)
        lax.fori_loop(0, (total % unroll + rest - 1) // rest, functools.partial(step, rest), item)

    mis_ref[...] = before_ref[...] + jnp.sum(acc_ref[...], axis=0)

    def finish(b, carry):
        result = (own_ref[b] + far_ref[b]) * (1.0 / W)
        out_ref[b] = scaled_rows(result, mis_ref[...]) if pack else result
        return carry

    lax.fori_loop(0, blocks, finish, 0, unroll=math.gcd(blocks, 2))


def band_call(limits, ok, before, x, firsts, wrap, pack):
    blocks, bins, rows, width = x.shape
    out_shape = (blocks, bins * 2 * W + EXTRA_ROWS, width) if pack else (blocks, bins, 2 * W, width)
    vmem = pl.BlockSpec(memory_space=pltpu.VMEM)
    smem = pl.BlockSpec(memory_space=pltpu.SMEM)
    return pl.pallas_call(
        functools.partial(band_kernel, firsts=firsts, wrap=wrap, pack=pack),
        out_shape=(
            jax.ShapeDtypeStruct(out_shape, jnp.float32),
            jax.ShapeDtypeStruct(before.shape, jnp.float32),
        ),
        in_specs=[smem, vmem, vmem, vmem],
        out_specs=(vmem, vmem),
        scratch_shapes=[
            pltpu.VMEM((blocks, bins, rows, 2 * width), jnp.bfloat16),
            pltpu.VMEM((blocks, bins, width, rows), jnp.bfloat16),
            pltpu.VMEM((bins, 8, 2 * width), jnp.float32),
            pltpu.VMEM((blocks, bins, 2 * W, width), jnp.float32),
            pltpu.VMEM((blocks, bins, 2 * W, width), jnp.float32),
            pltpu.VMEM((bins, width, 2 * width), jnp.bfloat16),
            pltpu.VMEM((bins, width, 2 * width), jnp.bfloat16),
            pltpu.VMEM((bins, width, 2 * width), jnp.bfloat16),
            pltpu.VMEM((bins, width, 2 * width), jnp.bfloat16),
        ],
        compiler_params=pltpu.CompilerParams(vmem_limit_bytes=40 * 2**20),
        name="band",
    )(limits, ok, before, x)


def sum_over(x, axis, reach=1):
    peers = lax.axis_size(axis)
    if reach == peers:
        return x
    if (peers // reach) & (peers // reach - 1):
        return lax.psum(x, axis) / reach
    while reach < peers:
        x = x + lax.ppermute(x, axis, [(i, i // (2 * reach) * 2 * reach + (i + reach) % (2 * reach)) for i in range(peers)])
        reach *= 2
    return x


def shards(spectra, model, channel_ok, limits):
    bin_total, _, _, width = spectra.shape
    peers = lax.axis_size("chan")
    here = lax.axis_index("chan")
    band_blocks = BAND // width
    group = max(g for g in range(1, peers + 1) if peers % g == 0 and bin_total % g == 0)
    wrap = group == peers
    groups = None if wrap else [[start + i for i in range(group)] for start in range(0, peers, group)]
    per_device = bin_total // group
    chunks = math.gcd(CHUNKS, per_device)
    bins = per_device // chunks
    chunk_bins = bin_total // chunks

    ok = channel_ok.reshape(peers, 1, width)
    ok_here = lax.dynamic_index_in_dim(ok, here, keepdims=False)
    if not wrap:
        start = here // group * group
        limits = lax.dynamic_slice_in_dim(limits, start, group)
        ok = lax.dynamic_slice_in_dim(jnp.concatenate([ok, ok]), start, group + band_blocks)
    arrays = spectra.reshape(bin_total, -1, width), model.reshape(bin_total, -1, width)
    rows = arrays[0].shape[1] + arrays[1].shape[1]

    def swap(x):
        return lax.all_to_all(x, "chan", 0, 0, axis_index_groups=groups, tiled=True)

    def halo_move(x, by):
        return lax.ppermute(x, "chan", [(i, (i + by) % peers) for i in range(peers)])

    adjoint, misfit = self_call(ok_here, *arrays)
    inbound = []
    after = misfit
    for c in range(chunks):
        if c:
            arrays, after = lax.optimization_barrier((arrays, after))
        inbound.append(swap(jnp.concatenate([x[c * chunk_bins : (c + 1) * chunk_bins] for x in arrays], axis=1)))
    outbound = []
    for c in range(chunks):
        part = inbound[c]
        if c:
            part, outbound[-1] = lax.optimization_barrier((part, outbound[-1]))
        part = part.reshape(group, bins, rows, width)
        if not wrap:
            part = jnp.concatenate([part, halo_move(part[:band_blocks], -group)], axis=0)
        packed, misfit = band_call(limits, ok, misfit, part, group, wrap, wrap)
        if not wrap:
            back = halo_move(packed[group:], group)
            packed = jnp.concatenate([packed[:band_blocks] + back, packed[band_blocks:group]], axis=0)
            packed = jax.vmap(scaled_rows, (0, None))(packed, misfit)
        outbound.append(packed.astype(jnp.float16))
    for c in range(chunks):
        packed = outbound[c]
        if c:
            packed, arrived = lax.optimization_barrier((packed, arrived))
        packed = swap(packed)
        arrived = packed
        part = unscaled(packed, bins).reshape(chunk_bins, 2 * W, width)
        part = part + lax.slice_in_dim(adjoint, c * chunk_bins, (c + 1) * chunk_bins)
        adjoint = lax.dynamic_update_slice_in_dim(adjoint, part, c * chunk_bins, 0)
    misfit = sum_over(sum_over(unscaled_misfit(packed), "freq"), "chan", group)
    misfit = misfit / float(2 * bin_total * lax.axis_size("freq") * peers * width * BAND)
    return adjoint.reshape(spectra.shape), misfit


def solution(mesh):
    return jax.shard_map(
        shards,
        mesh=mesh,
        in_specs=(P("freq", None, None, "chan"), P("freq", None, None, "chan"), P(), P()),
        out_specs=(P("freq", None, None, "chan"), P()),
        check_vma=False,
    )
```

```python
import functools
import math

import jax
import jax.numpy as jnp
from jax import lax
from jax.experimental import pallas as pl
from jax.experimental.pallas import tpu as pltpu
from jax.sharding import PartitionSpec as P

W = 16
BAND = 1024
CHUNKS = 2
UNROLL = 48
PREPARE_UNROLL = 8
FINISH_UNROLL = 4
REST = 16
SELF_UNROLL = 16
EXTRA_ROWS = 8
MISFIT_ROWS = 4


def power_below(top):
    return jnp.ceil(jnp.log(jnp.maximum(top, 1e-30)) * (1.0 / math.log(2.0)))


def scaled_rows(adjoint, misfit):
    bins, rows, width = adjoint.shape
    exponent = power_below(jnp.max(jnp.abs(adjoint), axis=1, keepdims=True))
    scaled = adjoint * jnp.exp2(15.0 - exponent)
    misfit = jnp.sum(misfit, axis=0, keepdims=True)
    misfit = misfit[:, :width] + misfit[:, width:]
    power = power_below(misfit)
    rest = misfit * jnp.exp2(10.0 - power)
    lines = [exponent[f] for f in range(bins)]
    lines += [jnp.zeros_like(misfit)] * (EXTRA_ROWS - MISFIT_ROWS - bins) + [power]
    for _ in range(2):
        lines.append(jnp.floor(rest))
        rest = (rest - jnp.floor(rest)) * 1024.0
    lines.append(rest)
    place = lax.broadcasted_iota(jnp.int32, (EXTRA_ROWS, width), 0)
    extra = jnp.zeros((EXTRA_ROWS, width), jnp.float32)
    for n, line in enumerate(lines):
        extra = jnp.where(place == n, line, extra)
    return jnp.concatenate([scaled.reshape(bins * rows, width), extra], axis=0)


def unscaled(packed, bins):
    blocks, _, width = packed.shape
    values = packed[:, : bins * 2 * W].astype(jnp.float32).reshape(blocks, bins, 2 * W, width)
    exponents = packed[:, bins * 2 * W : bins * 2 * W + bins].astype(jnp.float32)
    return values * jnp.exp2(exponents - 15.0)[:, :, None]


def unscaled_misfit(packed):
    power, high, middle, low = [packed[:, n - MISFIT_ROWS].astype(jnp.float32) for n in range(MISFIT_ROWS)]
    return jnp.sum((high + middle * 2.0**-10 + low * 2.0**-20) * jnp.exp2(power - 10.0))


def expanded(x):
    terms = (x.shape[0] - 2 * W) // 2
    sr, si, mr, mi = x[:W], x[W : 2 * W], x[2 * W : 2 * W + terms], x[2 * W + terms :]
    turned = jnp.concatenate([-si, sr, -mi, mr], axis=0)
    scaled = jnp.concatenate([x[: 2 * W] * (1.0 / W), -x[2 * W :]], axis=0)
    return x.astype(jnp.bfloat16), turned.astype(jnp.bfloat16), scaled.T.astype(jnp.bfloat16)


def squares(r):
    return jnp.sum((r * r).reshape(r.shape[0] // 8, 8, r.shape[1]), axis=0)


def apply_rows(w, r):
    return lax.dot_general(w[: 2 * W], r, (((1,), (1,)), ((), ())), preferred_element_type=jnp.float32)


def self_kernel(ok_ref, spectra_ref, model_ref, out_ref, mis_ref, *, unroll):
    bin_total, _, width = spectra_ref.shape
    row = lax.broadcasted_iota(jnp.int32, (width, 2 * width), 0)
    col = lax.broadcasted_iota(jnp.int32, (width, 2 * width), 1) % width
    ok = ok_ref[...].astype(jnp.float32)
    mis_ref[...] = jnp.zeros_like(mis_ref)

    def step(t, carry):
        total = jnp.zeros(mis_ref.shape, jnp.float32)
        for i in range(unroll):
            f = t * unroll + i
            x = jnp.concatenate([spectra_ref[f].astype(jnp.float32), model_ref[f].astype(jnp.float32)], axis=0) * ok
            x, turned, left = expanded(x)
            w = jnp.concatenate([x, turned], axis=1)
            r = jnp.dot(left, w, preferred_element_type=jnp.float32)
            r = jnp.where(row != col, r, 0.0)
            total += squares(r)
            out_ref[f] = apply_rows(w, r.astype(jnp.bfloat16)) * (1.0 / W)
        mis_ref[...] += total * 0.5
        return carry

    lax.fori_loop(0, bin_total // unroll, step, 0)


def self_call(ok, spectra, model):
    bin_total, _, width = spectra.shape
    vmem = pl.BlockSpec(memory_space=pltpu.VMEM)
    return pl.pallas_call(
        functools.partial(self_kernel, unroll=math.gcd(bin_total, SELF_UNROLL)),
        out_shape=(
            jax.ShapeDtypeStruct((bin_total, 2 * W, width), jnp.float32),
            jax.ShapeDtypeStruct((8, 2 * width), jnp.float32),
        ),
        in_specs=[vmem, vmem, vmem],
        out_specs=(vmem, vmem),
        compiler_params=pltpu.CompilerParams(vmem_limit_bytes=40 * 2**20),
        name="own_block",
    )(ok, spectra, model)


def band_kernel(limits_ref, ok_ref, before_ref, x_ref, out_ref, mis_ref, wt_ref, at_ref, acc_ref, own_ref, far_ref, r0_ref, r1_ref, t0_ref, t1_ref, live_ref, *, firsts, wrap, pack):
    blocks, bins, rows, width = x_ref.shape
    unroll = max(2, UNROLL // bins // 2 * 2)
    rest = max(2, REST // bins // 2 * 2)
    slots = (r0_ref, r1_ref)
    turned_slots = (t0_ref, t1_ref)
    acc_ref[...] = jnp.zeros_like(acc_ref)

    def prepare(b, carry):
        ok = ok_ref[b].astype(jnp.float32)
        for f in range(bins):
            x, turned, left = expanded(x_ref[b, f].astype(jnp.float32) * ok)
            wt_ref[b, f, :, :width] = x
            wt_ref[b, f, :, width:] = turned
            at_ref[b, f] = left
        own_ref[b] = jnp.zeros_like(own_ref[b])
        far_ref[b] = jnp.zeros_like(far_ref[b])
        return carry

    lax.fori_loop(0, blocks, prepare, 0, unroll=math.gcd(blocks, PREPARE_UNROLL))

    row = lax.broadcasted_iota(jnp.int32, (width, width), 0)
    col = lax.broadcasted_iota(jnp.int32, (width, width), 1)
    diff = col - row

    def last_piece(b):
        return (limits_ref[b] + width - 1) // width

    def next_item(b, s):
        done = (b >= firsts) | (s >= last_piece(jnp.minimum(b, firsts - 1)))
        return jnp.where(done, b + 1, b), jnp.where(done, 1, s + 1)

    def blocks_of(b, s):
        b = jnp.minimum(b, firsts - 1)
        j = b + s
        if wrap:
            j = jnp.where(j >= blocks, j - blocks, j)
        return b, j

    def cross(slot, item):
        b, s = item
        some = b < firsts
        b, j = blocks_of(b, s)
        live_ref[slot] = jnp.where(diff <= jnp.where(some, limits_ref[b] - s * width, -width), 1.0, 0.0)
        for f in range(bins):
            r = jnp.dot(at_ref[b, f], wt_ref[j, f], preferred_element_type=jnp.float32)
            live = live_ref[slot]
            r = jnp.concatenate([r[:, :width] * live, r[:, width:] * live], axis=1)
            acc_ref[f] += squares(r)
            r = r.astype(jnp.bfloat16)
            slots[slot][f] = r
            if f % 2:
                turned_slots[slot][f, :, :width] = r[:, :width].T
                turned_slots[slot][f, :, width:] = r[:, width:].T

    def adjoint(slot, item):
        b, j = blocks_of(*item)
        for f in range(bins):
            r = slots[slot][f]
            if f % 2:
                own = jnp.dot(wt_ref[j, f, : 2 * W, :width], turned_slots[slot][f], preferred_element_type=jnp.float32)
                own_ref[b, f, :W] += own[:W, :width] - own[W:, width:]
                own_ref[b, f, W:] += own[W:, :width] + own[:W, width:]
            else:
                own_ref[b, f] += apply_rows(wt_ref[j, f], r)
            far = jnp.dot(wt_ref[b, f, : 2 * W, :width], r, preferred_element_type=jnp.float32)
            far_ref[j, f, :W] += far[:W, :width] + far[W:, width:]
            far_ref[j, f, W:] += far[W:, :width] - far[:W, width:]

    def step(count, _, item):
        for i in range(count):
            later = next_item(*item)
            cross((i + 1) % 2, later)
            adjoint(i % 2, item)
            item = later
        return item

    total = lax.fori_loop(0, firsts, lambda b, n: n + last_piece(b), jnp.int32(0))
    first = (jnp.int32(0), jnp.int32(1))
    cross(0, first)
    if rest == unroll:
        lax.fori_loop(0, (total + unroll - 1) // unroll, functools.partial(step, unroll), first)
    else:
        item = lax.fori_loop(0, total // unroll, functools.partial(step, unroll), first)
        lax.fori_loop(0, (total % unroll + rest - 1) // rest, functools.partial(step, rest), item)

    mis_ref[...] = before_ref[...] + jnp.sum(acc_ref[...], axis=0)

    def finish(b, carry):
        result = (own_ref[b] + far_ref[b]) * (1.0 / W)
        out_ref[b] = scaled_rows(result, mis_ref[...]) if pack else result
        return carry

    lax.fori_loop(0, blocks, finish, 0, unroll=math.gcd(blocks, FINISH_UNROLL))


def band_call(limits, ok, before, x, firsts, wrap, pack):
    blocks, bins, rows, width = x.shape
    out_shape = (blocks, bins * 2 * W + EXTRA_ROWS, width) if pack else (blocks, bins, 2 * W, width)
    vmem = pl.BlockSpec(memory_space=pltpu.VMEM)
    smem = pl.BlockSpec(memory_space=pltpu.SMEM)
    return pl.pallas_call(
        functools.partial(band_kernel, firsts=firsts, wrap=wrap, pack=pack),
        out_shape=(
            jax.ShapeDtypeStruct(out_shape, jnp.float32),
            jax.ShapeDtypeStruct(before.shape, jnp.float32),
        ),
        in_specs=[smem, vmem, vmem, vmem],
        out_specs=(vmem, vmem),
        scratch_shapes=[
            pltpu.VMEM((blocks, bins, rows, 2 * width), jnp.bfloat16),
            pltpu.VMEM((blocks, bins, width, rows), jnp.bfloat16),
            pltpu.VMEM((bins, 8, 2 * width), jnp.float32),
            pltpu.VMEM((blocks, bins, 2 * W, width), jnp.float32),
            pltpu.VMEM((blocks, bins, 2 * W, width), jnp.float32),
            pltpu.VMEM((bins, width, 2 * width), jnp.bfloat16),
            pltpu.VMEM((bins, width, 2 * width), jnp.bfloat16),
            pltpu.VMEM((bins, width, 2 * width), jnp.bfloat16),
            pltpu.VMEM((bins, width, 2 * width), jnp.bfloat16),
            pltpu.VMEM((2, width, width), jnp.float32),
        ],
        compiler_params=pltpu.CompilerParams(vmem_limit_bytes=40 * 2**20),
        name="band",
    )(limits, ok, before, x)


def sum_over(x, axis, reach=1):
    peers = lax.axis_size(axis)
    if reach == peers:
        return x
    if (peers // reach) & (peers // reach - 1):
        return lax.psum(x, axis) / reach
    while reach < peers:
        x = x + lax.ppermute(x, axis, [(i, i // (2 * reach) * 2 * reach + (i + reach) % (2 * reach)) for i in range(peers)])
        reach *= 2
    return x


def shards(spectra, model, channel_ok, limits):
    bin_total, _, _, width = spectra.shape
    peers = lax.axis_size("chan")
    here = lax.axis_index("chan")
    band_blocks = BAND // width
    group = max(g for g in range(1, peers + 1) if peers % g == 0 and bin_total % g == 0)
    wrap = group == peers
    groups = None if wrap else [[start + i for i in range(group)] for start in range(0, peers, group)]
    per_device = bin_total // group
    chunks = math.gcd(CHUNKS, per_device)
    bins = per_device // chunks
    chunk_bins = bin_total // chunks

    ok = channel_ok.reshape(peers, 1, width)
    ok_here = lax.dynamic_index_in_dim(ok, here, keepdims=False)
    if not wrap:
        start = here // group * group
        limits = lax.dynamic_slice_in_dim(limits, start, group)
        ok = lax.dynamic_slice_in_dim(jnp.concatenate([ok, ok]), start, group + band_blocks)
    arrays = spectra.reshape(bin_total, -1, width), model.reshape(bin_total, -1, width)
    rows = arrays[0].shape[1] + arrays[1].shape[1]

    def swap(x):
        return lax.all_to_all(x, "chan", 0, 0, axis_index_groups=groups, tiled=True)

    def halo_move(x, by):
        return lax.ppermute(x, "chan", [(i, (i + by) % peers) for i in range(peers)])

    adjoint, misfit = self_call(ok_here, *arrays)
    inbound = []
    after = misfit
    for c in range(chunks):
        if c:
            arrays, after = lax.optimization_barrier((arrays, after))
        inbound.append(swap(jnp.concatenate([x[c * chunk_bins : (c + 1) * chunk_bins] for x in arrays], axis=1)))
    outbound = []
    for c in range(chunks):
        part = inbound[c]
        if c:
            part, outbound[-1] = lax.optimization_barrier((part, outbound[-1]))
        part = part.reshape(group, bins, rows, width)
        if not wrap:
            part = jnp.concatenate([part, halo_move(part[:band_blocks], -group)], axis=0)
        packed, misfit = band_call(limits, ok, misfit, part, group, wrap, wrap)
        if not wrap:
            back = halo_move(packed[group:], group)
            packed = jnp.concatenate([packed[:band_blocks] + back, packed[band_blocks:group]], axis=0)
            packed = jax.vmap(scaled_rows, (0, None))(packed, misfit)
        outbound.append(packed.astype(jnp.float16))
    for c in range(chunks):
        packed = outbound[c]
        if c:
            packed, arrived = lax.optimization_barrier((packed, arrived))
        packed = swap(packed)
        arrived = packed
        part = unscaled(packed, bins).reshape(chunk_bins, 2 * W, width)
        part = part + lax.slice_in_dim(adjoint, c * chunk_bins, (c + 1) * chunk_bins)
        adjoint = lax.dynamic_update_slice_in_dim(adjoint, part, c * chunk_bins, 0)
    misfit = sum_over(sum_over(unscaled_misfit(packed), "freq"), "chan", group)
    misfit = misfit / float(2 * bin_total * lax.axis_size("freq") * peers * width * BAND)
    return adjoint.reshape(spectra.shape), misfit


def solution(mesh):
    return jax.shard_map(
        shards,
        mesh=mesh,
        in_specs=(P("freq", None, None, "chan"), P("freq", None, None, "chan"), P(), P()),
        out_specs=(P("freq", None, None, "chan"), P()),
        check_vma=False,
    )
```

```python
import functools
import math

import jax
import jax.numpy as jnp
from jax import lax
from jax.experimental import pallas as pl
from jax.experimental.pallas import tpu as pltpu
from jax.sharding import PartitionSpec as P

W = 16
BAND = 1024
CHUNKS = 2
UNROLL = 48
PREPARE_UNROLL = 16
FINISH_UNROLL = 16
REST = 16
SELF_UNROLL = 16
EXTRA_ROWS = 8
MISFIT_ROWS = 4


def power_below(top):
    return jnp.ceil(jnp.log(jnp.maximum(top, 1e-30)) * (1.0 / math.log(2.0)))


def scaled_rows(adjoint, misfit):
    bins, rows, width = adjoint.shape
    exponent = power_below(jnp.max(jnp.abs(adjoint), axis=1, keepdims=True))
    scaled = adjoint * jnp.exp2(15.0 - exponent)
    misfit = jnp.sum(misfit, axis=0, keepdims=True)
    misfit = misfit[:, :width] + misfit[:, width:]
    power = power_below(misfit)
    rest = misfit * jnp.exp2(10.0 - power)
    lines = [exponent[f] for f in range(bins)]
    lines += [jnp.zeros_like(misfit)] * (EXTRA_ROWS - MISFIT_ROWS - bins) + [power]
    for _ in range(2):
        lines.append(jnp.floor(rest))
        rest = (rest - jnp.floor(rest)) * 1024.0
    lines.append(rest)
    place = lax.broadcasted_iota(jnp.int32, (EXTRA_ROWS, width), 0)
    extra = jnp.zeros((EXTRA_ROWS, width), jnp.float32)
    for n, line in enumerate(lines):
        extra = jnp.where(place == n, line, extra)
    return jnp.concatenate([scaled.reshape(bins * rows, width), extra], axis=0)


def unscaled(packed, bins):
    blocks, _, width = packed.shape
    values = packed[:, : bins * 2 * W].astype(jnp.float32).reshape(blocks, bins, 2 * W, width)
    exponents = packed[:, bins * 2 * W : bins * 2 * W + bins].astype(jnp.float32)
    return values * jnp.exp2(exponents - 15.0)[:, :, None]


def unscaled_misfit(packed):
    power, high, middle, low = [packed[:, n - MISFIT_ROWS].astype(jnp.float32) for n in range(MISFIT_ROWS)]
    return jnp.sum((high + middle * 2.0**-10 + low * 2.0**-20) * jnp.exp2(power - 10.0))


def expanded(x):
    terms = (x.shape[0] - 2 * W) // 2
    sr, si, mr, mi = x[:W], x[W : 2 * W], x[2 * W : 2 * W + terms], x[2 * W + terms :]
    turned = jnp.concatenate([-si, sr, -mi, mr], axis=0)
    scaled = jnp.concatenate([x[: 2 * W] * (1.0 / W), -x[2 * W :]], axis=0)
    return x.astype(jnp.bfloat16), turned.astype(jnp.bfloat16), scaled.T.astype(jnp.bfloat16)


def squares(r):
    return jnp.sum((r * r).reshape(r.shape[0] // 8, 8, r.shape[1]), axis=0)


def apply_rows(w, r):
    return lax.dot_general(w[: 2 * W], r, (((1,), (1,)), ((), ())), preferred_element_type=jnp.float32)


def self_kernel(ok_ref, spectra_ref, model_ref, out_ref, mis_ref, *, unroll):
    bin_total, _, width = spectra_ref.shape
    row = lax.broadcasted_iota(jnp.int32, (width, 2 * width), 0)
    col = lax.broadcasted_iota(jnp.int32, (width, 2 * width), 1) % width
    ok = ok_ref[...].astype(jnp.float32)
    mis_ref[...] = jnp.zeros_like(mis_ref)

    def step(t, carry):
        total = jnp.zeros(mis_ref.shape, jnp.float32)
        for i in range(unroll):
            f = t * unroll + i
            x = jnp.concatenate([spectra_ref[f].astype(jnp.float32), model_ref[f].astype(jnp.float32)], axis=0) * ok
            x, turned, left = expanded(x)
            w = jnp.concatenate([x, turned], axis=1)
            r = jnp.dot(left, w, preferred_element_type=jnp.float32)
            r = jnp.where(row != col, r, 0.0)
            total += squares(r)
            out_ref[f] = apply_rows(w, r.astype(jnp.bfloat16)) * (1.0 / W)
        mis_ref[...] += total * 0.5
        return carry

    lax.fori_loop(0, bin_total // unroll, step, 0)


def self_call(ok, spectra, model):
    bin_total, _, width = spectra.shape
    vmem = pl.BlockSpec(memory_space=pltpu.VMEM)
    return pl.pallas_call(
        functools.partial(self_kernel, unroll=math.gcd(bin_total, SELF_UNROLL)),
        out_shape=(
            jax.ShapeDtypeStruct((bin_total, 2 * W, width), jnp.float32),
            jax.ShapeDtypeStruct((8, 2 * width), jnp.float32),
        ),
        in_specs=[vmem, vmem, vmem],
        out_specs=(vmem, vmem),
        compiler_params=pltpu.CompilerParams(vmem_limit_bytes=40 * 2**20),
        name="own_block",
    )(ok, spectra, model)


def band_kernel(limits_ref, ok_ref, before_ref, x_ref, out_ref, mis_ref, wt_ref, at_ref, acc_ref, own_ref, far_ref, r0_ref, r1_ref, t0_ref, t1_ref, live_ref, *, firsts, wrap, pack):
    blocks, bins, rows, width = x_ref.shape
    unroll = max(2, UNROLL // bins // 2 * 2)
    rest = max(2, REST // bins // 2 * 2)
    slots = (r0_ref, r1_ref)
    turned_slots = (t0_ref, t1_ref)
    acc_ref[...] = jnp.zeros_like(acc_ref)

    def prepare(b, carry):
        ok = ok_ref[b].astype(jnp.float32)
        for f in range(bins):
            x, turned, left = expanded(x_ref[b, f].astype(jnp.float32) * ok)
            wt_ref[b, f, :, :width] = x
            wt_ref[b, f, :, width:] = turned
            at_ref[b, f] = left
        own_ref[b] = jnp.zeros_like(own_ref[b])
        far_ref[b] = jnp.zeros_like(far_ref[b])
        return carry

    lax.fori_loop(0, blocks, prepare, 0, unroll=math.gcd(blocks, PREPARE_UNROLL))

    row = lax.broadcasted_iota(jnp.int32, (width, width), 0)
    col = lax.broadcasted_iota(jnp.int32, (width, width), 1)
    diff = col - row

    def last_piece(b):
        return (limits_ref[b] + width - 1) // width

    def next_item(b, s):
        done = (b >= firsts) | (s >= last_piece(jnp.minimum(b, firsts - 1)))
        return jnp.where(done, b + 1, b), jnp.where(done, 1, s + 1)

    def blocks_of(b, s):
        b = jnp.minimum(b, firsts - 1)
        j = b + s
        if wrap:
            j = jnp.where(j >= blocks, j - blocks, j)
        return b, j

    def cross(slot, item):
        b, s = item
        some = b < firsts
        b, j = blocks_of(b, s)
        live_ref[slot] = jnp.where(diff <= jnp.where(some, limits_ref[b] - s * width, -width), 1.0, 0.0)
        for f in range(bins):
            r = jnp.dot(at_ref[b, f], wt_ref[j, f], preferred_element_type=jnp.float32)
            live = live_ref[slot]
            r = jnp.concatenate([r[:, :width] * live, r[:, width:] * live], axis=1)
            acc_ref[f] += squares(r)
            r = r.astype(jnp.bfloat16)
            slots[slot][f] = r
            if f % 2:
                turned_slots[slot][f, :, :width] = r[:, :width].T
                turned_slots[slot][f, :, width:] = r[:, width:].T

    def adjoint(slot, item):
        b, j = blocks_of(*item)
        for f in range(bins):
            r = slots[slot][f]
            if f % 2:
                own = jnp.dot(wt_ref[j, f, : 2 * W, :width], turned_slots[slot][f], preferred_element_type=jnp.float32)
                own_ref[b, f, :W] += own[:W, :width] - own[W:, width:]
                own_ref[b, f, W:] += own[W:, :width] + own[:W, width:]
            else:
                own_ref[b, f] += apply_rows(wt_ref[j, f], r)
            far = jnp.dot(wt_ref[b, f, : 2 * W, :width], r, preferred_element_type=jnp.float32)
            far_ref[j, f, :W] += far[:W, :width] + far[W:, width:]
            far_ref[j, f, W:] += far[W:, :width] - far[:W, width:]

    def step(count, _, item):
        for i in range(count):
            later = next_item(*item)
            cross((i + 1) % 2, later)
            adjoint(i % 2, item)
            item = later
        return item

    total = lax.fori_loop(0, firsts, lambda b, n: n + last_piece(b), jnp.int32(0))
    first = (jnp.int32(0), jnp.int32(1))
    cross(0, first)
    if rest == unroll:
        lax.fori_loop(0, (total + unroll - 1) // unroll, functools.partial(step, unroll), first)
    else:
        item = lax.fori_loop(0, total // unroll, functools.partial(step, unroll), first)
        lax.fori_loop(0, (total % unroll + rest - 1) // rest, functools.partial(step, rest), item)

    mis_ref[...] = before_ref[...] + jnp.sum(acc_ref[...], axis=0)

    def finish(b, carry):
        result = (own_ref[b] + far_ref[b]) * (1.0 / W)
        out_ref[b] = scaled_rows(result, mis_ref[...]) if pack else result
        return carry

    lax.fori_loop(0, blocks, finish, 0, unroll=math.gcd(blocks, FINISH_UNROLL))


def band_call(limits, ok, before, x, firsts, wrap, pack):
    blocks, bins, rows, width = x.shape
    out_shape = (blocks, bins * 2 * W + EXTRA_ROWS, width) if pack else (blocks, bins, 2 * W, width)
    vmem = pl.BlockSpec(memory_space=pltpu.VMEM)
    smem = pl.BlockSpec(memory_space=pltpu.SMEM)
    return pl.pallas_call(
        functools.partial(band_kernel, firsts=firsts, wrap=wrap, pack=pack),
        out_shape=(
            jax.ShapeDtypeStruct(out_shape, jnp.float32),
            jax.ShapeDtypeStruct(before.shape, jnp.float32),
        ),
        in_specs=[smem, vmem, vmem, vmem],
        out_specs=(vmem, vmem),
        scratch_shapes=[
            pltpu.VMEM((blocks, bins, rows, 2 * width), jnp.bfloat16),
            pltpu.VMEM((blocks, bins, width, rows), jnp.bfloat16),
            pltpu.VMEM((bins, 8, 2 * width), jnp.float32),
            pltpu.VMEM((blocks, bins, 2 * W, width), jnp.float32),
            pltpu.VMEM((blocks, bins, 2 * W, width), jnp.float32),
            pltpu.VMEM((bins, width, 2 * width), jnp.bfloat16),
            pltpu.VMEM((bins, width, 2 * width), jnp.bfloat16),
            pltpu.VMEM((bins, width, 2 * width), jnp.bfloat16),
            pltpu.VMEM((bins, width, 2 * width), jnp.bfloat16),
            pltpu.VMEM((2, width, width), jnp.float32),
        ],
        compiler_params=pltpu.CompilerParams(vmem_limit_bytes=40 * 2**20),
        name="band",
    )(limits, ok, before, x)


def sum_over(x, axis, reach=1):
    peers = lax.axis_size(axis)
    if reach == peers:
        return x
    if (peers // reach) & (peers // reach - 1):
        return lax.psum(x, axis) / reach
    while reach < peers:
        x = x + lax.ppermute(x, axis, [(i, i // (2 * reach) * 2 * reach + (i + reach) % (2 * reach)) for i in range(peers)])
        reach *= 2
    return x


def shards(spectra, model, channel_ok, limits):
    bin_total, _, _, width = spectra.shape
    peers = lax.axis_size("chan")
    here = lax.axis_index("chan")
    band_blocks = BAND // width
    group = max(g for g in range(1, peers + 1) if peers % g == 0 and bin_total % g == 0)
    wrap = group == peers
    groups = None if wrap else [[start + i for i in range(group)] for start in range(0, peers, group)]
    per_device = bin_total // group
    chunks = math.gcd(CHUNKS, per_device)
    bins = per_device // chunks
    chunk_bins = bin_total // chunks

    ok = channel_ok.reshape(peers, 1, width)
    ok_here = lax.dynamic_index_in_dim(ok, here, keepdims=False)
    if not wrap:
        start = here // group * group
        limits = lax.dynamic_slice_in_dim(limits, start, group)
        ok = lax.dynamic_slice_in_dim(jnp.concatenate([ok, ok]), start, group + band_blocks)
    arrays = spectra.reshape(bin_total, -1, width), model.reshape(bin_total, -1, width)
    rows = arrays[0].shape[1] + arrays[1].shape[1]

    def swap(x):
        return lax.all_to_all(x, "chan", 0, 0, axis_index_groups=groups, tiled=True)

    def halo_move(x, by):
        return lax.ppermute(x, "chan", [(i, (i + by) % peers) for i in range(peers)])

    adjoint, misfit = self_call(ok_here, *arrays)
    inbound = []
    after = misfit
    for c in range(chunks):
        if c:
            arrays, after = lax.optimization_barrier((arrays, after))
        inbound.append(swap(jnp.concatenate([x[c * chunk_bins : (c + 1) * chunk_bins] for x in arrays], axis=1)))
    outbound = []
    for c in range(chunks):
        part = inbound[c]
        if c:
            part, outbound[-1] = lax.optimization_barrier((part, outbound[-1]))
        part = part.reshape(group, bins, rows, width)
        if not wrap:
            part = jnp.concatenate([part, halo_move(part[:band_blocks], -group)], axis=0)
        packed, misfit = band_call(limits, ok, misfit, part, group, wrap, wrap)
        if not wrap:
            back = halo_move(packed[group:], group)
            packed = jnp.concatenate([packed[:band_blocks] + back, packed[band_blocks:group]], axis=0)
            packed = jax.vmap(scaled_rows, (0, None))(packed, misfit)
        outbound.append(packed.astype(jnp.float16))
    for c in range(chunks):
        packed = outbound[c]
        if c:
            packed, arrived = lax.optimization_barrier((packed, arrived))
        packed = swap(packed)
        arrived = packed
        part = unscaled(packed, bins).reshape(chunk_bins, 2 * W, width)
        part = part + lax.slice_in_dim(adjoint, c * chunk_bins, (c + 1) * chunk_bins)
        adjoint = lax.dynamic_update_slice_in_dim(adjoint, part, c * chunk_bins, 0)
    misfit = sum_over(sum_over(unscaled_misfit(packed), "freq"), "chan", group)
    misfit = misfit / float(2 * bin_total * lax.axis_size("freq") * peers * width * BAND)
    return adjoint.reshape(spectra.shape), misfit


def solution(mesh):
    return jax.shard_map(
        shards,
        mesh=mesh,
        in_specs=(P("freq", None, None, "chan"), P("freq", None, None, "chan"), P(), P()),
        out_specs=(P("freq", None, None, "chan"), P()),
        check_vma=False,
    )
```
